32 devices in a mesh: pipe: 8 (over z, core), dp: 4 (over y, x).
Axes of the slice: x: 2, y: 2, z: 4, core: 2. Of those that a mesh axis runs over, the one named last changes fastest.
Arguments:
- grads: bfloat16 [8, 2, 256, 8192], P('pipe', None, 'dp'), may hold values from -6 to 6
- weights: bfloat16 [8, 8192, 8192], P('pipe', 'dp'), may hold values from -0.0625 to 0.0625
- saved: bfloat16 [8, 3, 256, 8192], P('pipe', None, 'dp'), may hold values from -6 to 6
- plan: int32 [8, 2], P('pipe'), may hold values from 0 to 2, as said below
- block_of_section: int32 [8], P('pipe'), may hold values from 0 to 7, as said below
Outputs:
- upstream: bfloat16 [8, 2, 256, 8192], P('pipe', None, 'dp')
- inverse: bfloat16 [8, 512, 512], P('pipe')
The draws below stay inside these ranges and needn't reach their ends.
Inputs may be any that keep to these rules, and one draw needn't show every extreme that they name: `plan`: each row names 2 different slots. `block_of_section`: sections name distinct block numbers where 16 >= 8; otherwise every block number is named by 0 sections.
All inputs are finite; a program needn't handle non-finite values.
Results may differ from the reference program's by a relative error of at most 0.001.
Values may be sent and summed in bfloat16 or wider, within the bound.
A program may use at most 128 MiB of HBM per device.

```python
import jax
import jax.numpy as jnp
from jax import lax

D = 8192
BLK = 512
MB = 2
SAVED = 3
TOK = 256
N_PIPE = 8


def draw_plan(key, part):
    score_key = jax.random.fold_in(key, 11)
    row_key = jax.random.fold_in(key, 12)
    scores = jax.random.randint(score_key, (N_PIPE, SAVED), 0, 1 << 20) * SAVED + jnp.arange(SAVED, dtype=jnp.int32)[None, :]
    chosen_row = jax.random.randint(row_key, (), 0, N_PIPE)
    is_row = jnp.arange(N_PIPE, dtype=jnp.int32)[:, None] == chosen_row
    column = jnp.arange(SAVED, dtype=jnp.int32)[None, :]
    scores = jnp.where(is_row & (column == SAVED - 1), -2, scores)
    scores = jnp.where(is_row & (column == 0), -1, scores)
    order = jnp.argsort(scores, axis=1, stable=True)
    return order[:, :MB].astype(jnp.int32)


def draw_block_of_section(key, part):
    perm_key = jax.random.fold_in(key, 21)
    scores = jax.random.randint(perm_key, (N_PIPE,), 0, 1 << 20) * N_PIPE + jnp.arange(N_PIPE, dtype=jnp.int32)
    order = jnp.argsort(scores, stable=True).astype(jnp.int32)
    return order % (D // BLK)


def levels(rng, shape, pieces, low, largest):
    factor_of, own = 1.0, jax.random.fold_in(rng, 6)
    for axis_at, shards_of in pieces:
        steps = jnp.exp(jax.random.uniform(jax.random.fold_in(own, axis_at), (shards_of,), jnp.float32, low / len(pieces), largest / len(pieces)))
        factor_of = factor_of * jnp.repeat(steps, shape[axis_at] // shards_of).reshape([-1 if axis == axis_at else 1 for axis in range(len(shape))])
    return factor_of


def noise(key, dims, spread, bound, split=(), kind=jnp.bfloat16):
    factor_of = levels(key, dims, split, -0.22, 0.18) if split else 1.0
    drawn = jax.random.normal(key, dims, jnp.float32) * spread * factor_of
    return jnp.minimum(jnp.maximum(drawn, -bound), bound).astype(kind)


def setup_inputs(seed: int = 0) -> dict:
    keys = jax.random.split(jax.random.key(seed), 6)
    grads = noise(keys[0], (N_PIPE, MB, TOK, D), 1.0, 6.0, ((0, 8), (2, 4)))
    weights = noise(keys[1], (N_PIPE, D, D), D ** -0.5, 0.0625, ((0, 8), (1, 4)))
    saved = noise(keys[2], (N_PIPE, SAVED, TOK, D), 1.0, 6.0, ((0, 8), (2, 4)))
    plan = draw_plan(jax.random.fold_in(keys[5], 71), 0)
    block_of_section = draw_block_of_section(jax.random.fold_in(keys[5], 71), 0)
    return dict(grads=grads, weights=weights, saved=saved, plan=plan, block_of_section=block_of_section)


def invert_block(factor):
    lower = lax.linalg.cholesky(factor)
    eye = jnp.eye(factor.shape[0], dtype=jnp.float32)
    lower_inv = lax.linalg.triangular_solve(lower, eye, left_side=True, lower=True)
    return jnp.dot(lower_inv.T, lower_inv, precision=lax.Precision.HIGHEST).astype(jnp.bfloat16)

def one_section(packed):
    grad_section, weight_section, saved_section, slots, block = packed
    input_grad = jnp.einsum('mtd,id->mti', grad_section.astype(jnp.float32), weight_section.astype(jnp.float32)).astype(jnp.bfloat16)
    columns = lax.dynamic_slice_in_dim(saved_section, (block * BLK).astype(jnp.int32), BLK, 2)
    picked = jnp.take(columns, slots, axis=0).reshape(-1, BLK)
    gram = jnp.dot(picked.T.astype(jnp.float32), picked.astype(jnp.float32), preferred_element_type=jnp.float32)
    factor = gram / (MB * TOK) + jnp.eye(BLK, dtype=jnp.float32)
    return (input_grad, invert_block(factor))

def reference(grads, weights, saved, plan, block_of_section):
    input_grad, inverse = lax.map(one_section, (grads, weights, saved, plan, block_of_section))
    upstream = jnp.concatenate([input_grad[1:], jnp.zeros_like(input_grad[:1])], axis=0)
    return (upstream, inverse)
```

```python
import jax
import jax.numpy as jnp
from jax import lax
from jax.experimental import pallas as pl
from jax.experimental.pallas import tpu as pltpu
from jax.sharding import PartitionSpec as P

SUB = 8
LANES = 128


def three_parts(value):
    high = value.astype(jnp.bfloat16).astype(jnp.float32)
    rest = value - high
    mid = rest.astype(jnp.bfloat16).astype(jnp.float32)
    return high, mid, rest - mid


def exact_dot(a, b, contract):
    return lax.dot_general(
        a, b, (contract, ((), ())), precision=lax.Precision.HIGHEST, preferred_element_type=jnp.float32
    )


def invert_tile(tile):
    size = tile.shape[0]
    rows = [tile[at : at + SUB, :] for at in range(0, size, SUB)]
    lane = lax.broadcasted_iota(jnp.int32, (SUB, size), 1)
    sub = lax.broadcasted_iota(jnp.int32, (SUB, size), 0)
    for panel in range(size // SUB):
        first = panel * SUB
        old = rows[panel]
        inside = (lane >= first) & (lane < first + SUB)
        left = jnp.where(inside, 0.0, jnp.where(lane < first, -old, old))
        new = old
        for step in range(SUB):
            at = first + step
            column = jnp.broadcast_to(new[:, at : at + 1], new.shape)
            pivot = jnp.broadcast_to(column[step : step + 1, :], new.shape)
            cleared = jnp.where(lane == at, jnp.where(sub == step, 1.0, 0.0), new)
            row = jnp.broadcast_to(cleared[step : step + 1, :], new.shape) * (1.0 / pivot)
            new = jnp.where(sub == step, row, cleared - column * row)
        lh, lm, ll = three_parts(left)
        nh, nm, nl = three_parts(new)
        stacked_left = jnp.concatenate([lh, lh, lm, lh, lm, ll], axis=0).astype(jnp.bfloat16)
        stacked_new = jnp.concatenate([nh, nm, nh, nl, nm, nh], axis=0).astype(jnp.bfloat16)
        update = lax.dot_general(
            stacked_left, stacked_new, (((0,), (0,)), ((), ())), preferred_element_type=jnp.float32
        )
        rows = [
            new if at == panel else jnp.where(inside, 0.0, row) - update[at * SUB : (at + 1) * SUB, :]
            for at, row in enumerate(rows)
        ]
    return jnp.concatenate(rows, axis=0)


def invert_in_place(work):
    size = work.shape[0]

    def one_block(index, carry):
        at = pl.ds(pl.multiple_of(index * LANES, LANES), LANES)
        inverse = invert_tile(work[at, at])
        work[at, at] = jnp.zeros((LANES, LANES), jnp.float32)
        row = exact_dot(inverse, work[at, :], ((1,), (0,)))
        column = work[:, at]
        work[:, at] = jnp.zeros((size, LANES), jnp.float32)
        work[at, :] = row
        work[at, at] = inverse
        full = work[at, :]
        work[at, :] = jnp.zeros((LANES, size), jnp.float32)
        work[...] = work[...] - exact_dot(column, full, ((1,), (0,)))
        work[at, :] = full
        return carry

    lax.fori_loop(0, size // LANES, one_block, 0)


def inverse_kernel(rows_ref, out_ref, work):
    size = work.shape[0]
    gram = lax.dot_general(
        rows_ref[...], rows_ref[...], (((0,), (0,)), ((), ())), preferred_element_type=jnp.float32
    )
    down = lax.broadcasted_iota(jnp.int32, (size, size), 0)
    across = lax.broadcasted_iota(jnp.int32, (size, size), 1)
    work[...] = gram / rows_ref.shape[0] + jnp.where(down == across, 1.0, 0.0)
    invert_in_place(work)
    out_ref[...] = work[...].astype(out_ref.dtype)


def inverse_of(all_rows):
    size = all_rows.shape[1]
    return pl.pallas_call(
        inverse_kernel,
        out_shape=jax.ShapeDtypeStruct((size, size), jnp.bfloat16),
        scratch_shapes=[pltpu.VMEM((size, size), jnp.float32)],
        compiler_params=pltpu.CompilerParams(vmem_limit_bytes=24 * 1024 * 1024),
        cost_estimate=pl.CostEstimate(flops=10**9, bytes_accessed=150 * 10**6, transcendentals=0),
    )(all_rows)

BLK = 512


def passed_along(value, axis, steps):
    count = lax.axis_size(axis)
    first, last = (max(0, -steps), min(count, count - steps))
    return lax.ppermute(value, axis, [(source, source + steps) for source in range(first, last)])


def on_device(grads, weights, saved, plan, block_of_section):
    weight_rows = weights[0]
    columns = jnp.einsum(
        "amtd,id->amti",
        lax.all_gather(grads, "dp", axis=2, tiled=True),
        weight_rows,
        preferred_element_type=jnp.float32,
    ).astype(jnp.bfloat16)
    mine = lax.all_to_all(columns, "dp", split_axis=2, concat_axis=3, tiled=True)
    upstream = passed_along(mine, "pipe", -1)
    block = block_of_section[0]
    selected = lax.dynamic_slice_in_dim(saved[0], block * BLK, BLK, 2)
    picked = jnp.take(selected, plan[0], axis=0).reshape(-1, BLK)
    all_rows = lax.all_gather(picked, "dp", axis=0, tiled=True)
    inverse = inverse_of(all_rows)
    return (upstream, inverse[None])


def solution(mesh):
    in_specs = (
        P("pipe", None, "dp", None),
        P("pipe", "dp", None),
        P("pipe", None, "dp", None),
        P("pipe", None),
        P("pipe"),
    )
    out_specs = (P("pipe", None, "dp", None), P("pipe", None, None))
    return jax.shard_map(
        on_device, mesh=mesh, in_specs=in_specs, out_specs=out_specs, check_vma=False
    )
```

```python
import functools

import jax
import jax.numpy as jnp
from jax import lax
from jax.experimental import pallas as pl
from jax.experimental.pallas import tpu as pltpu
from jax.sharding import PartitionSpec as P

BLK = 512
SUB = 8
TILE = 256
PIECES = 2
LANES = 128


def three_parts(value):
    high = value.astype(jnp.bfloat16).astype(jnp.float32)
    rest = value - high
    mid = rest.astype(jnp.bfloat16).astype(jnp.float32)
    return high, mid, rest - mid


def exact_dot(a, b, contract):
    return lax.dot_general(
        a, b, (contract, ((), ())), precision=lax.Precision.HIGHEST, preferred_element_type=jnp.float32
    )


def invert_tile(tile):
    size = tile.shape[0]
    rows = [tile[at : at + SUB, :] for at in range(0, size, SUB)]
    lane = lax.broadcasted_iota(jnp.int32, (SUB, size), 1)
    sub = lax.broadcasted_iota(jnp.int32, (SUB, size), 0)
    spread = lambda value, at: jnp.broadcast_to(value[at : at + 1, :], value.shape)
    across = lambda value, at: jnp.broadcast_to(value[:, at : at + 1], value.shape)
    old = rows[0]
    for panel in range(size // SUB):
        first = panel * SUB
        inside = (lane >= first) & (lane < first + SUB)
        left = jnp.where(inside, 0.0, jnp.where(lane < first, -old, old))
        columns = [across(old, first + step) for step in range(SUB)]
        new = jnp.where(inside, jnp.where(lane - first == sub, 1.0, 0.0), old)
        for step in range(SUB):
            column = columns[step]
            scale = 1.0 / spread(column, step)
            here = sub == step

            def eliminate(value):
                row = spread(value, step) * scale
                return jnp.where(here, row, value - column * row)

            new = eliminate(new)
            for later in range(step + 1, SUB):
                columns[later] = eliminate(columns[later])
        if panel + 1 < size // SUB:
            following = rows[panel + 1]
            ahead = jnp.where(inside, 0.0, following)
            for step in range(SUB):
                ahead = ahead - across(following, first + step) * spread(new, step)
        lh, lm, ll = three_parts(left)
        nh, nm, nl = three_parts(new)
        stacked_left = jnp.concatenate([lh, lh, lm, lh, lm, ll], axis=0).astype(jnp.bfloat16)
        stacked_new = jnp.concatenate([nh, nm, nh, nl, nm, nh], axis=0).astype(jnp.bfloat16)
        update = lax.dot_general(
            stacked_left, stacked_new, (((0,), (0,)), ((), ())), preferred_element_type=jnp.float32
        )
        rows = [
            new if at == panel else jnp.where(inside, 0.0, row) - update[at * SUB : (at + 1) * SUB, :]
            for at, row in enumerate(rows)
        ]
        if panel + 1 < size // SUB:
            rows[panel + 1] = old = ahead
    return jnp.concatenate(rows, axis=0)


def invert_in_place(work):
    size = work.shape[0]

    def one_block(index, carry):
        at = pl.ds(pl.multiple_of(index * LANES, LANES), LANES)
        inverse = invert_tile(work[at, at])
        work[at, at] = jnp.zeros((LANES, LANES), jnp.float32)
        row = exact_dot(inverse, work[at, :], ((1,), (0,)))
        column = work[:, at]
        work[:, at] = jnp.zeros((size, LANES), jnp.float32)
        work[at, :] = row
        work[at, at] = inverse
        full = work[at, :]
        work[at, :] = jnp.zeros((LANES, size), jnp.float32)
        work[...] = work[...] - exact_dot(column, full, ((1,), (0,)))
        work[at, :] = full
        return carry

    lax.fori_loop(0, size // LANES, one_block, 0)


def relay_kernel(
    sections, peers, grads, weights, picked, upstream, inverse,
    shards, held, results, rows, work, zeros,
    own_sem, weight_sem, shard_send, shard_recv, row_send, row_recv, out_send, out_recv, zero_sem,
):
    section, me = lax.axis_index("pipe"), lax.axis_index("dp")
    micro, tokens, depth = shards.shape[1:]
    outs = held.shape[0]
    part = outs // PIECES
    tile = min(TILE, part)
    relayed = peers == 4

    def peer(slot):
        if relayed:
            return (me // 2 + slot // 2) % 2 * 2 + (me % 2 + slot % 2) % 2
        return (me + slot) % peers

    def beside(slot):
        return (section, peer(slot))

    barrier = pltpu.get_barrier_semaphore()
    for slot in range(1, peers):
        pl.semaphore_signal(barrier, inc=1, device_id=beside(slot), device_id_type=pl.DeviceIdType.MESH)

    for other in ((section + 1) % sections, (section + sections - 1) % sections):
        for slot in range(peers):
            pl.semaphore_signal(
                barrier, inc=1, device_id=(other, peer(slot)), device_id_type=pl.DeviceIdType.MESH
            )
    pl.semaphore_wait(barrier, 3 * peers - 1)

    def remote(source, target, send, recv, device):
        return pltpu.make_async_remote_copy(
            src_ref=source, dst_ref=target, send_sem=send, recv_sem=recv,
            device_id=device, device_id_type=pl.DeviceIdType.MESH,
        )

    def row_copy(slot):
        return remote(picked, rows.at[slot], row_send.at[slot], row_recv.at[slot], beside(slot))

    def shard_copy(slot, batch):
        return remote(
            grads.at[0, batch], shards.at[slot, batch],
            shard_send.at[slot, batch], shard_recv.at[slot, batch], beside(slot),
        )

    def relay_copy(batch):
        source, onward = (1, 2) if batch == 0 else (2, 1)
        return remote(
            shards.at[source, batch], shards.at[3, batch],
            shard_send.at[3, batch], shard_recv.at[3, batch], beside(onward),
        )

    def weight_copy(at):
        where = pl.ds(pl.multiple_of(at * tile, tile), tile)
        return pltpu.make_async_copy(weights.at[0, where, :], held.at[where, :], weight_sem.at[at])

    def result_copy(slot, piece):
        where = pl.ds(pl.multiple_of(me * outs + piece * part, part), part)
        return remote(
            results.at[slot, piece], upstream.at[0, :, :, where],
            out_send.at[slot, piece], out_recv.at[slot, piece], (section - 1, peer(slot)),
        )

    def zero_copy(at):
        return pltpu.make_async_copy(zeros, upstream.at[0, :, :, pl.ds(at * outs, outs)], zero_sem.at[at])

    for slot in range(1, peers):
        row_copy(slot).start()
    direct = range(1, 3) if relayed else range(1, peers)
    for turn in range(micro):
        for slot in direct:
            shard_copy(slot, turn if slot % 2 else micro - 1 - turn).start()
    own = pltpu.make_async_copy(grads.at[0], shards.at[0], own_sem.at[0])
    own.start()
    own_rows = pltpu.make_async_copy(picked, rows.at[0], own_sem.at[1])
    own_rows.start()
    lax.fori_loop(0, outs // tile, lambda at, carry: (weight_copy(at).start(), carry)[1], 0)

    @pl.when(section == sections - 1)
    def _():
        zeros[...] = jnp.zeros(zeros.shape, zeros.dtype)
        for at in range(peers):
            zero_copy(at).start()

    def multiply(first, count):
        for piece in range(PIECES):

            def one_tile(step, carry):
                at = piece * (part // tile) + step
                if first == 0:
                    weight_copy(at).wait()
                total = lax.dot_general(
                    shards[first : first + count].reshape(count * micro * tokens, depth),
                    held[pl.ds(pl.multiple_of(at * tile, tile), tile), :],
                    (((1,), (1,)), ((), ())),
                    preferred_element_type=jnp.float32,
                )
                results[first : first + count, piece, :, :, pl.ds(pl.multiple_of(step * tile, tile), tile)] = (
                    total.astype(results.dtype).reshape(count, micro, tokens, tile)
                )
                return carry

            lax.fori_loop(0, part // tile, one_tile, 0)

            @pl.when(section > 0)
            def _():
                for slot in range(first, first + count):
                    result_copy(slot, piece).start()

    own.wait()
    multiply(0, 1)

    own_rows.wait()
    for slot in range(1, peers):
        row_copy(slot).wait_recv()
    size = work.shape[0]
    flat = rows[...].reshape(-1, size)
    gram = lax.dot_general(flat, flat, (((0,), (0,)), ((), ())), preferred_element_type=jnp.float32)
    down = lax.broadcasted_iota(jnp.int32, (size, size), 0)
    along = lax.broadcasted_iota(jnp.int32, (size, size), 1)
    work[...] = gram / flat.shape[0] + jnp.where(down == along, 1.0, 0.0)
    invert_in_place(work)
    inverse[0] = work[...].astype(inverse.dtype)

    arrived = set()

    def arrive(slot, batch):
        if (slot, batch) not in arrived:
            arrived.add((slot, batch))
            shard_copy(slot, batch).wait_recv()

    if relayed:
        for batch in range(micro):
            arrive(1 if batch == 0 else 2, batch)
            relay_copy(batch).start()
    at = 1
    while at < peers:
        count = min(2, peers - at)
        for slot in range(at, at + count):
            for batch in range(micro):
                arrive(slot, batch)
        multiply(at, count)
        at += count

    for slot in range(1, peers):
        row_copy(slot).wait_send()
        for batch in range(micro):
            shard_copy(slot, batch).wait_send()

    @pl.when(section > 0)
    def _():
        for slot in range(peers):
            for piece in range(PIECES):
                result_copy(slot, piece).wait_send()

    @pl.when(section < sections - 1)
    def _():
        for slot in range(peers):
            for piece in range(PIECES):
                result_copy(slot, piece).wait_recv()

    @pl.when(section == sections - 1)
    def _():
        for at in range(peers):
            zero_copy(at).wait()


def relay(sections, peers, grads, weights, picked):
    micro, tokens, depth = grads.shape[1:]
    outs = weights.shape[1]
    part = outs // PIECES
    size = picked.shape[1]
    dma = pltpu.SemaphoreType.DMA
    anywhere = pl.BlockSpec(memory_space=pl.ANY)
    return pl.pallas_call(
        functools.partial(relay_kernel, sections, peers),
        out_shape=(
            jax.ShapeDtypeStruct(grads.shape, grads.dtype),
            jax.ShapeDtypeStruct((1, size, size), jnp.bfloat16),
        ),
        in_specs=[anywhere] * 3,
        out_specs=(anywhere, pl.BlockSpec(memory_space=pltpu.VMEM)),
        scratch_shapes=[
            pltpu.VMEM((peers, micro, tokens, depth), grads.dtype),
            pltpu.VMEM((outs, depth), weights.dtype),
            pltpu.VMEM((peers, PIECES, micro, tokens, part), grads.dtype),
            pltpu.VMEM((peers,) + picked.shape, picked.dtype),
            pltpu.VMEM((size, size), jnp.float32),
            pltpu.VMEM((micro, tokens, outs), grads.dtype),
            dma((2,)),
            dma((outs // min(TILE, part),)),
            dma((peers, micro)),
            dma((peers, micro)),
            dma((peers,)),
            dma((peers,)),
            dma((peers, PIECES)),
            dma((peers, PIECES)),
            dma((peers,)),
        ],
        compiler_params=pltpu.CompilerParams(
            collective_id=0, has_side_effects=True, vmem_limit_bytes=58 * 1024 * 1024
        ),
        cost_estimate=pl.CostEstimate(
            flops=2 * peers * micro * tokens * outs * depth,
            bytes_accessed=2 * outs * depth,
            transcendentals=0,
        ),
    )(grads, weights, picked)


def on_device(grads, weights, saved, plan, block_of_section):
    tokens = saved.shape[2]
    column = block_of_section[0] * BLK
    picked = jnp.concatenate(
        [
            lax.dynamic_slice(saved, (0, plan[0, batch], 0, column), (1, 1, tokens, BLK))[0, 0]
            for batch in range(plan.shape[1])
        ],
        axis=0,
    )
    return relay(lax.axis_size("pipe"), lax.axis_size("dp"), grads, weights, picked)


def solution(mesh):
    in_specs = (
        P("pipe", None, "dp", None),
        P("pipe", "dp", None),
        P("pipe", None, "dp", None),
        P("pipe", None),
        P("pipe"),
    )
    out_specs = (P("pipe", None, "dp", None), P("pipe", None, None))
    return jax.shard_map(
        on_device, mesh=mesh, in_specs=in_specs, out_specs=out_specs, check_vma=False
    )
```

```python
import functools

import jax
import jax.numpy as jnp
from jax import lax
from jax.experimental import pallas as pl
from jax.experimental.pallas import tpu as pltpu
from jax.sharding import PartitionSpec as P

BLK = 512
SUB = 8
TILE = 256
PIECES = 4
LANES = 128


def three_parts(value):
    high = value.astype(jnp.bfloat16).astype(jnp.float32)
    rest = value - high
    mid = rest.astype(jnp.bfloat16).astype(jnp.float32)
    return high, mid, rest - mid


def exact_dot(a, b, contract):
    return lax.dot_general(
        a, b, (contract, ((), ())), precision=lax.Precision.HIGHEST, preferred_element_type=jnp.float32
    )


def invert_tile(tile):
    size = tile.shape[0]
    rows = [tile[at : at + SUB, :] for at in range(0, size, SUB)]
    lane = lax.broadcasted_iota(jnp.int32, (SUB, size), 1)
    sub = lax.broadcasted_iota(jnp.int32, (SUB, size), 0)
    spread = lambda value, at: jnp.broadcast_to(value[at : at + 1, :], value.shape)
    across = lambda value, at: jnp.broadcast_to(value[:, at : at + 1], value.shape)
    old = rows[0]
    for panel in range(size // SUB):
        first = panel * SUB
        inside = (lane >= first) & (lane < first + SUB)
        left = jnp.where(inside, 0.0, jnp.where(lane < first, -old, old))
        columns = [across(old, first + step) for step in range(SUB)]
        new = jnp.where(inside, jnp.where(lane - first == sub, 1.0, 0.0), old)
        for step in range(SUB):
            column = columns[step]
            scale = 1.0 / spread(column, step)
            here = sub == step

            def eliminate(value):
                row = spread(value, step) * scale
                return jnp.where(here, row, value - column * row)

            new = eliminate(new)
            for later in range(step + 1, SUB):
                columns[later] = eliminate(columns[later])
        if panel + 1 < size // SUB:
            following = rows[panel + 1]
            ahead = jnp.where(inside, 0.0, following)
            for step in range(SUB):
                ahead = ahead - across(following, first + step) * spread(new, step)
        lh, lm, ll = three_parts(left)
        nh, nm, nl = three_parts(new)
        stacked_left = jnp.concatenate([lh, lh, lm, lh, lm, ll], axis=0).astype(jnp.bfloat16)
        stacked_new = jnp.concatenate([nh, nm, nh, nl, nm, nh], axis=0).astype(jnp.bfloat16)
        update = lax.dot_general(
            stacked_left, stacked_new, (((0,), (0,)), ((), ())), preferred_element_type=jnp.float32
        )
        rows = [
            new if at == panel else jnp.where(inside, 0.0, row) - update[at * SUB : (at + 1) * SUB, :]
            for at, row in enumerate(rows)
        ]
        if panel + 1 < size // SUB:
            rows[panel + 1] = old = ahead
    return jnp.concatenate(rows, axis=0)


def eliminate_blocks(work, first, end):
    size = work.shape[0]

    def one_block(index, carry):
        at = pl.ds(pl.multiple_of(index * LANES, LANES), LANES)
        inverse = invert_tile(work[at, at])
        work[at, at] = jnp.zeros((LANES, LANES), jnp.float32)
        row = exact_dot(inverse, work[at, :], ((1,), (0,)))
        column = work[:, at]
        work[:, at] = jnp.zeros((size, LANES), jnp.float32)
        work[at, :] = row
        work[at, at] = inverse
        full = work[at, :]
        work[at, :] = jnp.zeros((LANES, size), jnp.float32)
        work[...] = work[...] - exact_dot(column, full, ((1,), (0,)))
        work[at, :] = full
        return carry

    lax.fori_loop(first, end, one_block, 0)


def relay_kernel(
    sections, peers, grads, weights, picked, upstream, inverse,
    shards, held, results, rows, work, zeros,
    own_sem, weight_sem, shard_send, shard_recv, row_sem, row_send, row_recv, out_send, out_recv, zero_sem,
):
    section, me = lax.axis_index("pipe"), lax.axis_index("dp")
    micro, tokens, depth = shards.shape[1:]
    outs = held.shape[0]
    part = outs // PIECES
    tile = min(TILE, part)
    relayed = peers == 4

    def peer(slot):
        if relayed:
            return (me // 2 + slot // 2) % 2 * 2 + (me % 2 + slot % 2) % 2
        return (me + slot) % peers

    def beside(slot):
        return (section, peer(slot))

    own_rows = pltpu.make_async_copy(picked, rows.at[0], row_sem)
    own_rows.start()
    own = pltpu.make_async_copy(grads.at[0], shards.at[0], own_sem)
    own.start()

    barrier = pltpu.get_barrier_semaphore()
    for slot in range(1, peers):
        pl.semaphore_signal(barrier, inc=1, device_id=beside(slot), device_id_type=pl.DeviceIdType.MESH)

    for other in ((section + 1) % sections, (section + sections - 1) % sections):
        for slot in range(peers):
            pl.semaphore_signal(
                barrier, inc=1, device_id=(other, peer(slot)), device_id_type=pl.DeviceIdType.MESH
            )
    pl.semaphore_wait(barrier, 3 * peers - 1)

    def remote(source, target, send, recv, device):
        return pltpu.make_async_remote_copy(
            src_ref=source, dst_ref=target, send_sem=send, recv_sem=recv,
            device_id=device, device_id_type=pl.DeviceIdType.MESH,
        )

    def row_copy(slot):
        return remote(picked, rows.at[slot], row_send.at[slot], row_recv.at[slot], beside(slot))

    def shard_copy(slot, batch):
        return remote(
            grads.at[0, batch], shards.at[slot, batch],
            shard_send.at[slot, batch], shard_recv.at[slot, batch], beside(slot),
        )

    def relay_copy(batch):
        source, onward = (1, 2) if batch == 0 else (2, 1)
        return remote(
            shards.at[source, batch], shards.at[3, batch],
            shard_send.at[3, batch], shard_recv.at[3, batch], beside(onward),
        )

    def weight_copy(at):
        where = pl.ds(pl.multiple_of(at * tile, tile), tile)
        return pltpu.make_async_copy(weights.at[0, where, :], held.at[where, :], weight_sem.at[at])

    def result_copy(slot, piece):
        where = pl.ds(pl.multiple_of(me * outs + piece * part, part), part)
        return remote(
            results.at[slot, piece], upstream.at[0, :, :, where],
            out_send.at[slot, piece], out_recv.at[slot, piece], (section - 1, peer(slot)),
        )

    def zero_copy(at):
        return pltpu.make_async_copy(zeros, upstream.at[0, :, :, pl.ds(at * outs, outs)], zero_sem.at[at])

    def send_shards(turn):
        for slot in range(1, 3) if relayed else range(1, peers):
            shard_copy(slot, turn if slot % 2 else micro - 1 - turn).start()

    for slot in range(1, peers):
        row_copy(slot).start()
    send_shards(0)
    lax.fori_loop(0, outs // tile, lambda at, carry: (weight_copy(at).start(), carry)[1], 0)

    @pl.when(section == sections - 1)
    def _():
        zeros[...] = jnp.zeros(zeros.shape, zeros.dtype)
        for at in range(peers):
            zero_copy(at).start()

    def multiply(first, count):
        for piece in range(PIECES):

            def one_tile(step, carry):
                at = piece * (part // tile) + step
                if first == 0:
                    weight_copy(at).wait()
                total = lax.dot_general(
                    shards[first : first + count].reshape(count * micro * tokens, depth),
                    held[pl.ds(pl.multiple_of(at * tile, tile), tile), :],
                    (((1,), (1,)), ((), ())),
                    preferred_element_type=jnp.float32,
                )
                results[first : first + count, piece, :, :, pl.ds(pl.multiple_of(step * tile, tile), tile)] = (
                    total.astype(results.dtype).reshape(count, micro, tokens, tile)
                )
                return carry

            lax.fori_loop(0, part // tile, one_tile, 0)

            @pl.when(section > 0)
            def _():
                for slot in range(first, first + count):
                    result_copy(slot, piece).start()

    own.wait()
    multiply(0, 1)
    for turn in range(1, micro):
        send_shards(turn)

    own_rows.wait()
    for slot in range(1, peers):
        row_copy(slot).wait_recv()
    size = work.shape[0]
    flat = rows[...].reshape(-1, size)
    gram = lax.dot_general(flat, flat, (((0,), (0,)), ((), ())), preferred_element_type=jnp.float32)
    down = lax.broadcasted_iota(jnp.int32, (size, size), 0)
    along = lax.broadcasted_iota(jnp.int32, (size, size), 1)
    work[...] = gram / flat.shape[0] + jnp.where(down == along, 1.0, 0.0)
    blocks = size // LANES
    eliminate_blocks(work, 0, blocks // 2)

    arrived = set()

    def arrive(slot, batch):
        if (slot, batch) not in arrived:
            arrived.add((slot, batch))
            shard_copy(slot, batch).wait_recv()

    if relayed:
        for batch in range(micro):
            arrive(1 if batch == 0 else 2, batch)
            relay_copy(batch).start()
    eliminate_blocks(work, blocks // 2, blocks - 1)
    at = 1
    while at < peers:
        count = min(2, peers - at)
        for slot in range(at, at + count):
            for batch in range(micro):
                arrive(slot, batch)
        multiply(at, count)
        at += count

    eliminate_blocks(work, blocks - 1, blocks)
    inverse[0] = work[...].astype(inverse.dtype)
    for slot in range(1, peers):
        row_copy(slot).wait_send()
        for batch in range(micro):
            shard_copy(slot, batch).wait_send()

    @pl.when(section > 0)
    def _():
        for slot in range(peers):
            for piece in range(PIECES):
                result_copy(slot, piece).wait_send()

    @pl.when(section < sections - 1)
    def _():
        for slot in range(peers):
            for piece in range(PIECES):
                result_copy(slot, piece).wait_recv()

    @pl.when(section == sections - 1)
    def _():
        for at in range(peers):
            zero_copy(at).wait()


def relay(sections, peers, grads, weights, picked):
    micro, tokens, depth = grads.shape[1:]
    outs = weights.shape[1]
    part = outs // PIECES
    size = BLK
    dma = pltpu.SemaphoreType.DMA
    anywhere = pl.BlockSpec(memory_space=pl.ANY)
    return pl.pallas_call(
        functools.partial(relay_kernel, sections, peers),
        out_shape=(
            jax.ShapeDtypeStruct(grads.shape, grads.dtype),
            jax.ShapeDtypeStruct((1, size, size), jnp.bfloat16),
        ),
        in_specs=[anywhere] * 3,
        out_specs=(anywhere, pl.BlockSpec(memory_space=pltpu.VMEM)),
        scratch_shapes=[
            pltpu.VMEM((peers, micro, tokens, depth), grads.dtype),
            pltpu.VMEM((outs, depth), weights.dtype),
            pltpu.VMEM((peers, PIECES, micro, tokens, part), grads.dtype),
            pltpu.VMEM((peers,) + picked.shape, picked.dtype),
            pltpu.VMEM((size, size), jnp.float32),
            pltpu.VMEM((micro, tokens, outs), grads.dtype),
            dma,
            dma((outs // min(TILE, part),)),
            dma((peers, micro)),
            dma((peers, micro)),
            dma,
            dma((peers,)),
            dma((peers,)),
            dma((peers, PIECES)),
            dma((peers, PIECES)),
            dma((peers,)),
        ],
        compiler_params=pltpu.CompilerParams(
            collective_id=0, has_side_effects=True, vmem_limit_bytes=58 * 1024 * 1024
        ),
        cost_estimate=pl.CostEstimate(
            flops=2 * peers * micro * tokens * outs * depth,
            bytes_accessed=2 * outs * depth,
            transcendentals=0,
        ),
    )(grads, weights, picked)


def copy_kernel(first, second, first_out, second_out, sems):
    copies = [
        pltpu.make_async_copy(first, first_out, sems.at[0]),
        pltpu.make_async_copy(second, second_out, sems.at[1]),
    ]
    for copy in copies:
        copy.start()
    for copy in copies:
        copy.wait()


def handed_over(first, second):
    anywhere = pl.BlockSpec(memory_space=pl.ANY)
    return pl.pallas_call(
        copy_kernel,
        out_shape=(
            jax.ShapeDtypeStruct(first.shape, first.dtype),
            jax.ShapeDtypeStruct(second.shape, second.dtype),
        ),
        in_specs=[anywhere] * 2,
        out_specs=(anywhere, anywhere),
        scratch_shapes=[pltpu.SemaphoreType.DMA((2,))],
        compiler_params=pltpu.CompilerParams(vmem_limit_bytes=58 * 1024 * 1024),
    )(first, second)


def pick_kernel(plan, block, saved, picked, sems):
    micro, tokens = plan.shape[1], saved.shape[2]
    column = pl.ds(pl.multiple_of(block[0] * BLK, BLK), BLK)
    copies = [
        pltpu.make_async_copy(
            saved.at[0, plan[0, batch], :, column], picked.at[pl.ds(batch * tokens, tokens), :], sems.at[batch]
        )
        for batch in range(micro)
    ]
    for copy in copies:
        copy.start()
    for copy in copies:
        copy.wait()


def pick(saved, plan, block):
    anywhere = pl.BlockSpec(memory_space=pl.ANY)
    scalars = pl.BlockSpec(memory_space=pltpu.SMEM)
    return pl.pallas_call(
        pick_kernel,
        out_shape=jax.ShapeDtypeStruct((plan.shape[1] * saved.shape[2], BLK), saved.dtype),
        in_specs=[scalars, scalars, anywhere],
        out_specs=anywhere,
        scratch_shapes=[pltpu.SemaphoreType.DMA((plan.shape[1],))],
        compiler_params=pltpu.CompilerParams(vmem_limit_bytes=58 * 1024 * 1024),
    )(plan, block, saved)


def on_device(grads, weights, saved, plan, block_of_section):
    picked = pick(saved, plan, block_of_section)
    return handed_over(*relay(lax.axis_size("pipe"), lax.axis_size("dp"), grads, weights, picked))


def solution(mesh):
    in_specs = (
        P("pipe", None, "dp", None),
        P("pipe", "dp", None),
        P("pipe", None, "dp", None),
        P("pipe", None),
        P("pipe"),
    )
    out_specs = (P("pipe", None, "dp", None), P("pipe", None, None))
    return jax.shard_map(
        on_device, mesh=mesh, in_specs=in_specs, out_specs=out_specs, check_vma=False
    )
```
